256 devices in a mesh: fsdp: 64 (over x, z, core), rep: 4 (over y).
Axes of the slice: x: 4, y: 4, z: 8, core: 2. Of those that a mesh axis runs over, the one named last changes fastest.
Arguments:
- hidden_rows: bfloat16 [32768, 5120], P(('rep', 'fsdp')), parts along dimension 0, may hold values from -6 to 6
- queries: bfloat16 [32768, 4096], P(('rep', 'fsdp')), parts along dimension 0, may hold values from -6 to 6
- norm_gain: float32 [5120], replicated, may hold values from 0.1 to 1.9
- query_gain: float32 [128], replicated, may hold values from 0.5 to 12
- key_norm_gain: float32 [128], replicated, may hold values from 0.5 to 2
- key_matrix: bfloat16 [5120, 512], P('fsdp'), may hold values from -0.078125 to 0.078125
- value_matrix: bfloat16 [5120, 512], P('fsdp'), may hold values from -0.078125 to 0.078125
- lengths: int32 [256], P('rep'), parts along dimension 0, may hold values from 1 to 256, as said below
- owner: int32 [256], P('rep'), parts along dimension 0, may hold values from 0 to 63, as said below
Outputs:
- context: bfloat16 [32768, 4096], P(('rep', 'fsdp')), parts along dimension 0
The draws below stay inside these ranges and needn't reach their ends.
There are 4 independent parts, one for each index of `rep`. The reference program is written for one: setup_inputs(seed, part) draws one part's arguments, and reference() takes and returns one part's arrays. A program takes and returns all parts, laid end to end along the dimension named above; an argument that names none is the same for every part. Nothing has to cross between parts.
Inputs may be any that keep to these rules, and one draw needn't show every extreme that they name: The lengths sum to 8192; one rollout has exactly 256 tokens. The rollouts of one owner hold at most 256 tokens together; some owner holds exactly 256.
All inputs are finite; a program needn't handle non-finite values.
Results may differ from the reference program's by a relative error of at most 0.012.
The reference program's roundings to bfloat16 on the way count: a program that leaves them out, or rounds other values in their place, can miss the bound.
Values may be sent and summed in bfloat16 or wider, within the bound.
No kernel may reach another device: no remote copies, remote signals or barrier semaphores. Data moves between devices by JAX's collectives and lax.ppermute only.
A program may use at most 128 MiB of HBM per device.

```python
import math
import jax
import jax.numpy as jnp
from jax import lax

MODEL_WIDTH = 5120
HQ = 32
KEY_VALUE_HEADS = 4
HEAD_SIZE = 128
TOK_DEV = 128
QUERY_GROUP_SIZE = 8
LONGEST_ROLLOUT = 256
NSEQ = 64
BATCH_TOKENS = 8192


def rollout_plan(key):
    tail = BATCH_TOKENS - LONGEST_ROLLOUT
    pieces = NSEQ - 1
    stride = tail // pieces
    inner = jnp.arange(1, pieces, dtype=jnp.int32)
    bases = inner * tail // pieces
    jitter = jax.random.randint(jax.random.fold_in(key, 11), (pieces - 1,), 0, stride)
    cuts = jnp.concatenate([jnp.zeros((1,), jnp.int32), (bases + jitter).astype(jnp.int32), jnp.full((1,), tail, jnp.int32)])
    rest = (cuts[1:] - cuts[:-1]).astype(jnp.int32)
    ordered = jnp.concatenate([jnp.full((1,), LONGEST_ROLLOUT, jnp.int32), rest])
    shuffle = jax.random.permutation(jax.random.fold_in(key, 12), NSEQ)
    lengths = ordered[shuffle].astype(jnp.int32)
    index = jnp.arange(NSEQ, dtype=jnp.int32)
    order = jnp.argsort(-(lengths * NSEQ + index), stable=True).astype(jnp.int32)

    def place(step, state):
        owner_rows, squares, assigned = state
        sequence = order[step]
        length = lengths[sequence]
        room = owner_rows + length <= LONGEST_ROLLOUT
        target = jnp.argmin(jnp.where(room, squares, 2 ** 30)).astype(jnp.int32)
        owner_rows = owner_rows.at[target].add(length)
        squares = squares.at[target].add(length * length)
        assigned = assigned.at[sequence].set(target)
        return (owner_rows, squares, assigned)
    start = (jnp.zeros((NSEQ,), jnp.int32), jnp.zeros((NSEQ,), jnp.int32), jnp.zeros((NSEQ,), jnp.int32))
    owners = lax.fori_loop(0, NSEQ, place, start)[2]
    return (lengths, owners)


def draw_lengths(key, part):
    plan = rollout_plan(key)
    return plan[0]


def draw_owner(key, part):
    plan = rollout_plan(key)
    return plan[1]


def draw_query_gain(key, part):
    key = jax.random.fold_in(key, 5)
    unit = jax.random.uniform(key, (HEAD_SIZE,), jnp.float32)
    return jnp.exp(jnp.log(0.5) + unit * (jnp.log(2.0) - jnp.log(0.5))).astype(jnp.float32)


def block_levels(rng, shape, split, low, high):
    level = 1.0
    for axis_at, blocks in split:
        draws = jax.random.uniform(jax.random.fold_in(jax.random.fold_in(rng, 6), axis_at), (blocks,), jnp.float32, low / len(split), high / len(split))
        level = level * jnp.repeat(jnp.exp(draws), shape[axis_at] // blocks).reshape((-1,) + (1,) * (len(shape) - 1 - axis_at))
    return level


def noise(stream_key, extent, scale, limit, cuts=(), held_as=jnp.bfloat16):
    values = jax.random.normal(stream_key, extent, jnp.float32) * scale
    if len(cuts) > 0:
        values = block_levels(stream_key, extent, cuts, -0.22, 0.18) * values
    return jnp.clip(values, min=-limit, max=limit).astype(held_as)


def setup_inputs(seed: int = 0, part: int = 0) -> dict:
    streams_of = jax.random.split(jax.random.key(seed), 10)
    own_keys = jax.random.split(jax.random.fold_in(streams_of[9], part), 10)
    hidden_rows = noise(own_keys[0], (BATCH_TOKENS, MODEL_WIDTH), 1.0, 6.0, ((0, 64),))
    queries = noise(own_keys[1], (BATCH_TOKENS, HQ * HEAD_SIZE), 1.0, 6.0, ((0, 64),))
    norm_gain = jnp.clip(1.0 + 0.18 * jax.random.normal(streams_of[2], (MODEL_WIDTH,), jnp.float32), 0.1, 1.9)
    query_gain = draw_query_gain(jax.random.fold_in(streams_of[9], 71), part)
    key_norm_gain = jnp.clip(jnp.exp(jax.random.uniform(streams_of[4], (HEAD_SIZE,), jnp.float32, math.log(0.5), math.log(2.0))), 0.5, 2.0)
    key_matrix = noise(streams_of[5], (MODEL_WIDTH, KEY_VALUE_HEADS * HEAD_SIZE), MODEL_WIDTH ** -0.5, 0.078125, ((0, 64),))
    value_matrix = noise(streams_of[6], (MODEL_WIDTH, KEY_VALUE_HEADS * HEAD_SIZE), MODEL_WIDTH ** -0.5, 0.078125, ((0, 64),))
    lengths = draw_lengths(jax.random.fold_in(jax.random.fold_in(streams_of[9], part), 71), part)
    owner = draw_owner(jax.random.fold_in(jax.random.fold_in(streams_of[9], part), 71), part)
    return dict(hidden_rows=hidden_rows, queries=queries, norm_gain=norm_gain, query_gain=query_gain, key_norm_gain=key_norm_gain, key_matrix=key_matrix, value_matrix=value_matrix, lengths=lengths, owner=owner)


eps = 1e-06
rope_base = 1000000.0

def root_mean_norm(value_rows, gain):
    mean_square = lax.optimization_barrier(jnp.mean(value_rows * value_rows, axis=-1, keepdims=True))
    return value_rows * lax.rsqrt(mean_square + eps) * gain

def apply_rotary(value_rows, token_positions):
    half = value_rows.shape[-1] // 2
    steps = jnp.arange(half, dtype=jnp.float32) * (2.0 / value_rows.shape[-1])
    inverse = jnp.power(jnp.float32(rope_base), -steps)
    angles = token_positions.astype(jnp.float32)[:, None] * inverse[None, :]
    cosine = jnp.cos(angles)[:, None, :]
    sine = jnp.sin(angles)[:, None, :]
    first = value_rows[..., :half]
    second = value_rows[..., half:]
    return jnp.concatenate([first * cosine - second * sine, second * cosine + first * sine], axis=-1)

def offsets_of(lengths, owner):
    index = jnp.arange(lengths.shape[0], dtype=jnp.int32)
    earlier = (owner[None, :] < owner[:, None]) | (owner[None, :] == owner[:, None]) & (index[None, :] < index[:, None])
    return lax.optimization_barrier(jnp.sum(jnp.where(earlier, lengths[None, :], 0), axis=1)).astype(jnp.int32)

def token_info(tokens, offset, lengths):
    index = jnp.arange(lengths.shape[0], dtype=jnp.int32)
    member = (tokens[:, None] >= offset[None, :]) & (tokens[:, None] < (offset + lengths)[None, :])
    sequence = lax.optimization_barrier(jnp.sum(jnp.where(member, index[None, :], 0), axis=1)).astype(jnp.int32)
    start = lax.optimization_barrier(jnp.sum(jnp.where(member, offset[None, :], 0), axis=1)).astype(jnp.int32)
    return (sequence, (tokens - start).astype(jnp.int32))

def reference(hidden_rows, queries, norm_gain, query_gain, key_norm_gain, key_matrix, value_matrix, lengths, owner):
    order = jnp.arange(BATCH_TOKENS, dtype=jnp.int32)
    row_of = (order % NSEQ * TOK_DEV + order // NSEQ).astype(jnp.int32)
    offset = offsets_of(lengths, owner)
    sequence, token_positions = token_info(order, offset, lengths)
    normed = root_mean_norm(hidden_rows[row_of].astype(jnp.float32), norm_gain).astype(jnp.bfloat16)
    unnormed_keys = jnp.dot(normed, key_matrix, preferred_element_type=jnp.float32)
    value_rows = jnp.dot(normed, value_matrix, preferred_element_type=jnp.float32).astype(jnp.bfloat16)
    key_rows = apply_rotary(root_mean_norm(unnormed_keys.reshape(BATCH_TOKENS, KEY_VALUE_HEADS, HEAD_SIZE), key_norm_gain), token_positions).astype(jnp.bfloat16)
    prepared_heads = apply_rotary(root_mean_norm(queries[row_of].astype(jnp.float32).reshape(BATCH_TOKENS, HQ, HEAD_SIZE), query_gain), token_positions).astype(jnp.bfloat16)
    prepared_heads = prepared_heads.reshape(BATCH_TOKENS, KEY_VALUE_HEADS, QUERY_GROUP_SIZE, HEAD_SIZE)
    padded_keys = jnp.concatenate([jnp.zeros((LONGEST_ROLLOUT, KEY_VALUE_HEADS, HEAD_SIZE), jnp.bfloat16), key_rows], axis=0)
    padded_values = jnp.concatenate([jnp.zeros((LONGEST_ROLLOUT, KEY_VALUE_HEADS, HEAD_SIZE), jnp.bfloat16), value_rows.reshape(BATCH_TOKENS, KEY_VALUE_HEADS, HEAD_SIZE)], axis=0)
    seq_pad = jnp.concatenate([jnp.full((LONGEST_ROLLOUT,), -1, jnp.int32), sequence])
    pos_pad = jnp.concatenate([jnp.zeros((LONGEST_ROLLOUT,), jnp.int32), token_positions])

    def block(number):
        start = (number * LONGEST_ROLLOUT).astype(jnp.int32)
        query_block = lax.dynamic_slice_in_dim(prepared_heads, start, LONGEST_ROLLOUT, 0).astype(jnp.float32)
        query_seq = lax.dynamic_slice_in_dim(sequence, start, LONGEST_ROLLOUT, 0)
        query_pos = lax.dynamic_slice_in_dim(token_positions, start, LONGEST_ROLLOUT, 0)
        key_block = lax.dynamic_slice_in_dim(padded_keys, start, 2 * LONGEST_ROLLOUT, 0).astype(jnp.float32)
        value_block = lax.dynamic_slice_in_dim(padded_values, start, 2 * LONGEST_ROLLOUT, 0).astype(jnp.float32)
        key_seq = lax.dynamic_slice_in_dim(seq_pad, start, 2 * LONGEST_ROLLOUT, 0)
        key_pos = lax.dynamic_slice_in_dim(pos_pad, start, 2 * LONGEST_ROLLOUT, 0)
        allowed = (query_seq[:, None] == key_seq[None, :]) & (key_pos[None, :] <= query_pos[:, None])
        scores = jnp.einsum('qhgd,khd->hgqk', query_block, key_block) / jnp.sqrt(jnp.float32(HEAD_SIZE))
        scores = jnp.where(allowed[None, None], scores, -jnp.inf)
        top = lax.optimization_barrier(jnp.max(scores, axis=-1, keepdims=True))
        weights = jnp.exp(scores - top)
        probs = (weights / lax.optimization_barrier(jnp.sum(weights, axis=-1, keepdims=True))).astype(jnp.bfloat16)
        mixed = jnp.einsum('hgqk,khd->qhgd', probs.astype(jnp.float32), value_block)
        return mixed.astype(jnp.bfloat16).reshape(LONGEST_ROLLOUT, HQ * HEAD_SIZE)
    ordered = lax.map(block, jnp.arange(BATCH_TOKENS // LONGEST_ROLLOUT, dtype=jnp.int32)).reshape(BATCH_TOKENS, HQ * HEAD_SIZE)
    owner_rows = jnp.arange(BATCH_TOKENS, dtype=jnp.int32)
    token_of = (owner_rows % TOK_DEV * NSEQ + owner_rows // TOK_DEV).astype(jnp.int32)
    return ordered[token_of]
```

```python
import functools

import jax
import jax.numpy as jnp
import numpy as np
from jax import lax
from jax.experimental import pallas as pl
from jax.experimental.pallas import tpu as pltpu
from jax.sharding import Mesh, PartitionSpec as P

NX, NZ, NC = 4, 8, 2
NF = NX * NZ * NC
WIDTH = 5120
HEADS = 8
HEAD = 128
ROWS = 128
SHARD = WIDTH // NF
RNG = 8
HALO = 4
KROWS = RNG + HALO
QTOK = NF * RNG
KTOK = NF * KROWS
X_ORDER = (0, -1, 1, 2)
Z_ORDER = (0, -1, 1, -2, 2, -3, 3, 4)

eps = 1e-06
rope_base = 1000000.0
BF = jnp.bfloat16
F32 = jnp.float32


def shift(value, axis, size, by):
    return lax.ppermute(value, axis, [(i, (i + by) % size) for i in range(size)])


def rollout_starts(lengths, owner, tokens):
    index = jnp.arange(lengths.shape[0], dtype=jnp.int32)
    earlier = (owner[None, :] < owner[:, None]) | (owner[None, :] == owner[:, None]) & (
        index[None, :] < index[:, None]
    )
    offset = jnp.sum(jnp.where(earlier, lengths[None, :], 0), axis=1)
    return jnp.max(jnp.where(offset[None, :] <= tokens[:, None], offset[None, :], 0), axis=1)


def rope_tables(positions):
    half = HEAD // 2
    steps = jnp.arange(half, dtype=F32) * (2.0 / HEAD)
    inverse = jnp.power(F32(rope_base), -steps)
    angles = positions.astype(F32)[:, None] * inverse[None, :]
    cosine = jnp.cos(angles)
    sine = jnp.sin(angles)
    return (
        jnp.concatenate([cosine, cosine], axis=1),
        jnp.concatenate([-sine, sine], axis=1),
    )


def normed_rope(value, gain, cosine, sine):
    mean_square = jnp.mean(value * value, axis=-1, keepdims=True)
    value = value * lax.rsqrt(mean_square + eps) * gain
    return value * cosine + pltpu.roll(value, HEAD // 2, 1) * sine


def project_kernel(
    place, own, left, right, far_a, far_b, mine, other, gain, cosine, sine, out, weight, keep_k, keep_v, sem
):
    z, c = place[1], place[2]
    copies = []
    for k, by in enumerate(Z_ORDER):
        at = lax.rem(z + by + NZ, NZ)
        for which, core in ((mine, c), (other, 1 - c)):
            copies.append(
                pltpu.make_async_copy(
                    which.at[k], weight.at[:, at, core], sem.at[len(copies)]
                )
            )
    for copy in copies:
        copy.start()
    for copy in copies:
        copy.wait()
    w = weight[...].reshape(WIDTH, 2 * HEAD)
    for k in range(NX):
        x = (
            (own, left, right)[k][...]
            if k < 3
            else jnp.concatenate([far_a[...], far_b[...]], axis=0)
        )
        raw = jnp.dot(x, w, preferred_element_type=F32)
        rows = pl.ds(k * ROWS, ROWS)
        key = normed_rope(raw[:, :HEAD], gain[...], cosine[rows, :], sine[rows, :])
        keep_k[pl.ds(k, ROWS, stride=NX), :] = key
        keep_v[pl.ds(k, ROWS, stride=NX), :] = raw[:, HEAD:]
    out[0, : NX * HALO, :] = jnp.zeros((NX * HALO, 2 * HEAD), BF)
    for keep, lanes in ((keep_k, pl.ds(0, HEAD)), (keep_v, pl.ds(HEAD, HEAD))):
        out[0, NX * HALO :, lanes] = keep[: NX * RNG, :].astype(BF)
        for j in range(1, NZ * NC):
            start = NX * (RNG * j - HALO)
            out[j, :, lanes] = keep[start : start + NX * KROWS, :].astype(BF)


def prepare_kernel(q, gain, cosine, sine, out):
    value = q[...].astype(F32)
    out[...] = normed_rope(value, gain[...], cosine[...], sine[...]).astype(BF)


def attend_kernel(q, kv, token, start, key_token, out, bias, scores, probs):
    @pl.when(pl.program_id(0) == 0)
    def _():
        seen = (key_token[...] >= start[...]) & (key_token[...] <= token[...])
        bias[...] = jnp.where(seen, 0.0, -jnp.inf)

    keys = kv[:, :HEAD]
    values = kv[:, HEAD:]
    scores[...] = lax.dot_general(
        q[...], keys, (((1,), (1,)), ((), ())), preferred_element_type=F32
    )
    block = 64

    def body(i, carry):
        rows = pl.ds(pl.multiple_of(i * block, block), block)
        s = scores[rows, :] * (1.0 / np.sqrt(HEAD)).astype(np.float32) + bias[rows, :]
        top = jnp.max(s, axis=1, keepdims=True)
        weights = jnp.exp(s - top)
        total = jnp.sum(weights, axis=1, keepdims=True)
        probs[rows, :] = (weights / total).astype(BF)
        return carry

    lax.fori_loop(0, QTOK // block, body, 0)
    out[...] = jnp.dot(probs[...], values, preferred_element_type=F32).astype(BF)


def per_device(
    hidden_rows,
    queries,
    norm_gain,
    query_gain,
    key_norm_gain,
    key_matrix,
    value_matrix,
    lengths,
    owner,
):
    x, z, c = (lax.axis_index(a).astype(jnp.int32) for a in ("x", "z", "core"))
    zc = z * NC + c
    place = jnp.stack([x, z, c])
    fsdp = ("x", "z", "core")

    hidden = hidden_rows.astype(F32)
    mean_square = jnp.mean(hidden * hidden, axis=-1, keepdims=True)
    normed = (hidden * lax.rsqrt(mean_square + eps) * norm_gain).astype(BF)
    left = shift(normed, "x", NX, 1)
    right = shift(normed, "x", NX, -1)

    packed = jnp.concatenate(
        [key_matrix.reshape(SHARD, NX, 1, HEAD), value_matrix.reshape(SHARD, NX, 1, HEAD)], axis=2
    )
    packed = packed.transpose(1, 0, 2, 3).reshape(NX, SHARD, 2 * HEAD)
    piece = lax.all_to_all(packed, "x", split_axis=0, concat_axis=0, tiled=True)
    pieces = [piece]
    up = down = piece
    for _ in range(NZ // 2 - 1):
        up = shift(up, "z", NZ, 1)
        down = shift(down, "z", NZ, -1)
        pieces += [up, down]
    half = NX // 2
    pieces.append(
        jnp.concatenate(
            [shift(up[:half], "z", NZ, 1), shift(down[half:], "z", NZ, -1)], axis=0
        )
    )
    mine = jnp.stack(pieces)
    other = shift(mine, "core", NC, 1)

    far_a = shift(left[: ROWS // 2], "x", NX, 1)
    far_b = shift(right[ROWS // 2 :], "x", NX, -1)

    sent = queries.reshape(NZ * NC, RNG, NX, HEADS * HEAD).transpose(2, 0, 1, 3)
    sent = sent.reshape(NF, RNG, HEADS * HEAD)
    got = lax.all_to_all(sent, fsdp, split_axis=0, concat_axis=0, tiled=True)

    rows = jnp.arange(ROWS, dtype=jnp.int32)
    chunk_x = jnp.stack([(x + by + NX) % NX for by in X_ORDER])
    made = (rows[None, :] * NF + chunk_x[:, None] * (NZ * NC) + zc).reshape(-1)
    key_cos, key_sin = rope_tables(made - rollout_starts(lengths, owner, made))
    token = (
        (zc * RNG + jnp.arange(RNG, dtype=jnp.int32))[None, :] * NF
        + jnp.arange(NF, dtype=jnp.int32)[:, None]
    ).reshape(-1)
    start = rollout_starts(lengths, owner, token)
    q_cos, q_sin = rope_tables(token - start)
    key_rows = zc * RNG - HALO + jnp.arange(KROWS, dtype=jnp.int32)
    key_token = (
        key_rows[None, :, None] * NF
        + chunk_x[None, None, :] * (NZ * NC)
        + jnp.arange(NZ * NC, dtype=jnp.int32)[:, None, None]
    ).reshape(1, KTOK)

    ready = pl.pallas_call(
        prepare_kernel,
        grid=(HEADS,),
        in_specs=[
            pl.BlockSpec((QTOK, HEAD), lambda h: (0, h)),
            pl.BlockSpec((1, HEAD), lambda h: (0, 0)),
            pl.BlockSpec((QTOK, HEAD), lambda h: (0, 0)),
            pl.BlockSpec((QTOK, HEAD), lambda h: (0, 0)),
        ],
        out_specs=pl.BlockSpec((QTOK, HEAD), lambda h: (0, h)),
        out_shape=jax.ShapeDtypeStruct((QTOK, HEADS * HEAD), BF),
        name="prepare_queries",
    )(got.reshape(QTOK, HEADS * HEAD), query_gain.reshape(1, HEAD), q_cos, q_sin)

    vmem = pl.BlockSpec(memory_space=pltpu.VMEM)
    anywhere = pl.BlockSpec(memory_space=pl.ANY)
    made_kv = pl.pallas_call(
        project_kernel,
        in_specs=[pl.BlockSpec(memory_space=pltpu.SMEM)]
        + [vmem] * 5
        + [anywhere] * 2
        + [vmem] * 3,
        out_specs=vmem,
        out_shape=jax.ShapeDtypeStruct((NZ * NC, NX * KROWS, 2 * HEAD), BF),
        scratch_shapes=[
            pltpu.VMEM((NX, NZ, NC, SHARD, 2 * HEAD), BF),
            pltpu.VMEM((NX * ROWS, HEAD), F32),
            pltpu.VMEM((NX * ROWS, HEAD), F32),
            pltpu.SemaphoreType.DMA((2 * NZ,)),
        ],
        compiler_params=pltpu.CompilerParams(vmem_limit_bytes=40 * 2**20),
        name="project_keys_values",
    )(
        place,
        normed,
        left,
        right,
        far_a,
        far_b,
        mine,
        other,
        key_norm_gain.reshape(1, HEAD),
        key_cos,
        key_sin,
    )
    kv = lax.all_to_all(made_kv, ("z", "core"), split_axis=0, concat_axis=0, tiled=True)

    mixed = pl.pallas_call(
        attend_kernel,
        grid=(HEADS,),
        in_specs=[
            pl.BlockSpec((QTOK, HEAD), lambda h: (0, h)),
            pl.BlockSpec((KTOK, 2 * HEAD), lambda h: (0, 0)),
            pl.BlockSpec((QTOK, 1), lambda h: (0, 0)),
            pl.BlockSpec((QTOK, 1), lambda h: (0, 0)),
            pl.BlockSpec((1, KTOK), lambda h: (0, 0)),
        ],
        out_specs=pl.BlockSpec((QTOK, HEAD), lambda h: (0, h)),
        out_shape=jax.ShapeDtypeStruct((QTOK, HEADS * HEAD), BF),
        scratch_shapes=[
            pltpu.VMEM((QTOK, KTOK), F32),
            pltpu.VMEM((QTOK, KTOK), F32),
            pltpu.VMEM((QTOK, KTOK), BF),
        ],
        compiler_params=pltpu.CompilerParams(vmem_limit_bytes=32 * 2**20),
        name="attend",
    )(ready, kv.reshape(KTOK, 2 * HEAD), token[:, None], start[:, None], key_token)

    back = lax.all_to_all(
        mixed.reshape(NF, RNG, HEADS * HEAD), fsdp, split_axis=0, concat_axis=0, tiled=True
    )
    back = back.reshape(NX, NZ * NC, RNG, HEADS * HEAD).transpose(1, 2, 0, 3)
    return back.reshape(ROWS, NX * HEADS * HEAD)


def solution(mesh):
    grid = Mesh(mesh.devices.reshape(NX, NZ, NC, mesh.devices.shape[1]), ("x", "z", "core", "rep"))
    fsdp = ("x", "z", "core")
    whole = P(("rep",) + fsdp, None)
    placed = (whole, whole, P(), P(), P(), P(fsdp, None), P(fsdp, None), P("rep"), P("rep"))
    return jax.shard_map(
        per_device, mesh=grid, in_specs=placed, out_specs=whole, check_vma=False
    )
```

```python
import functools

import jax
import jax.numpy as jnp
import numpy as np
from jax import lax
from jax.experimental import pallas as pl
from jax.experimental.pallas import tpu as pltpu
from jax.sharding import Mesh, PartitionSpec as P

NX, NZ, NC = 4, 8, 2
NF = NX * NZ * NC
WIDTH = 5120
HEADS = 8
HEAD = 128
ROWS = 128
SHARD = WIDTH // NF
RNG = 8
HALO = 4
KROWS = RNG + HALO
QTOK = NF * RNG
KTOK = NF * KROWS
PAIR = 2 * NF
WINDOW = (HALO + 2) * NF
X_ORDER = (0, -1, 1, 2)
Z_ORDER = (0, -1, 1, -2, 2, -3, 3, 4)
NEAR = 5

eps = 1e-06
rope_base = 1000000.0
BF = jnp.bfloat16
F32 = jnp.float32


def shift(value, axis, size, by):
    return lax.ppermute(value, axis, [(i, (i + by) % size) for i in range(size)])


def rollout_starts(lengths, owner, tokens):
    index = jnp.arange(lengths.shape[0], dtype=jnp.int32)
    earlier = (owner[None, :] < owner[:, None]) | (owner[None, :] == owner[:, None]) & (
        index[None, :] < index[:, None]
    )
    offset = jnp.sum(jnp.where(earlier, lengths[None, :], 0), axis=1)
    return jnp.max(jnp.where(offset[None, :] <= tokens[:, None], offset[None, :], 0), axis=1)


def rope_tables(positions):
    half = HEAD // 2
    steps = jnp.arange(half, dtype=F32) * (2.0 / HEAD)
    inverse = jnp.power(F32(rope_base), -steps)
    angles = positions.astype(F32)[:, None] * inverse[None, :]
    cosine = jnp.cos(angles)
    sine = jnp.sin(angles)
    return (
        jnp.concatenate([cosine, cosine], axis=1),
        jnp.concatenate([-sine, sine], axis=1),
    )


def normed_rope(value, gain, cosine, sine):
    mean_square = jnp.mean(value * value, axis=-1, keepdims=True)
    value = value * lax.rsqrt(mean_square + eps) * gain
    return value * cosine + pltpu.roll(value, HEAD // 2, 1) * sine


def pack_kernel(place, key, value, *out):
    for k, by in enumerate(X_ORDER):
        head = lax.rem(place[0] - by + NX, NX)
        lanes = pl.ds(pl.multiple_of(head * HEAD, HEAD), HEAD)
        out[k][:, :HEAD] = key[:, lanes]
        out[k][:, HEAD:] = value[:, lanes]


def norm_kernel(hidden, gain, top, low):
    block = 16
    for out, base in ((top, 0), (low, ROWS // 2)):
        for i in range(0, ROWS // 2, block):
            value = hidden[base + i : base + i + block, :].astype(F32)
            mean_square = jnp.mean(value * value, axis=-1, keepdims=True)
            value = value * lax.rsqrt(mean_square + eps) * gain[...]
            out[i : i + block, :] = value.astype(BF)


def project(x, w, gain, cosine, sine):
    raw = jnp.dot(x, w, preferred_element_type=F32)
    return normed_rope(raw[:, :HEAD], gain, cosine, sine), raw[:, HEAD:]


def first_kernel(
    place,
    own_a,
    own_b,
    left_a,
    left_b,
    right_a,
    right_b,
    mine,
    mine2,
    other,
    other2,
    gain,
    cosine,
    sine,
    out,
    weight,
    sem,
):
    x, z, c = place[0], place[1], place[2]
    copies = []
    for k, by in enumerate(Z_ORDER):
        at = lax.rem(z + by + NZ, NZ)
        near = k < NEAR
        for which, core in (((mine, mine2)[k >= NEAR], c), ((other, other2)[k >= NEAR], 1 - c)):
            for i, step in enumerate(X_ORDER):
                copies.append(
                    pltpu.make_async_copy(
                        which.at[k if near else k - NEAR, i],
                        weight.at[lax.rem(x + step + NX, NX), at, core],
                        sem.at[len(copies)],
                    )
                )
    for copy in copies:
        copy.start()
    for copy in copies:
        copy.wait()
    w = weight[...].reshape(WIDTH, 2 * HEAD)
    for k in range(NX - 1):
        top, low = ((own_a, own_b), (left_a, left_b), (right_a, right_b))[k]
        tokens = jnp.concatenate([top[...], low[...]], axis=0)
        rows = pl.ds(k * ROWS, ROWS)
        key, value = project(tokens, w, gain[...], cosine[rows, :], sine[rows, :])
        out[k, 0] = key
        out[k, 1] = value


def second_kernel(far_a, far_b, weight, made, gain, cosine, sine, out, keep_k, keep_v):
    w = weight[...].reshape(WIDTH, 2 * HEAD)
    x = jnp.concatenate([far_a[...], far_b[...]], axis=0)
    rows = pl.ds((NX - 1) * ROWS, ROWS)
    far = project(x, w, gain[...], cosine[rows, :], sine[rows, :])
    for side, (keep, lanes) in enumerate(((keep_k, pl.ds(0, HEAD)), (keep_v, pl.ds(HEAD, HEAD)))):
        for k in range(NX - 1):
            keep[pl.ds(k, ROWS, stride=NX), :] = made[k, side]
        keep[pl.ds(NX - 1, ROWS, stride=NX), :] = far[side]
        out[0, : NX * HALO, lanes] = jnp.zeros((NX * HALO, HEAD), BF)
        out[0, NX * HALO :, lanes] = keep[: NX * RNG, :].astype(BF)
        for j in range(1, NZ * NC):
            start = NX * (RNG * j - HALO)
            out[j, :, lanes] = keep[start : start + NX * KROWS, :].astype(BF)


def prepare_kernel(q, gain, cosine, sine, out, wide):
    for h in range(HEADS):
        wide[h] = q[:, pl.ds(h * HEAD, HEAD)].astype(F32)
    for r in range(RNG):
        rows = pl.ds(r * NF, NF)
        for h in range(HEADS):
            value = wide[h, pl.ds(r, NF, stride=RNG), :]
            value = normed_rope(value, gain[...], cosine[rows, :], sine[rows, :])
            out[r // 2, pl.ds(h * PAIR + (r % 2) * NF, NF), :] = value.astype(BF)


def attend_kernel(q, kv, token, start, key_token, out, bias, kept, mixed, probs, scores):
    wide = kv[...].astype(F32)
    for i in range(KROWS // 2):
        part = wide[:, 2 * NX * i : 2 * NX * (i + 1), :].reshape(PAIR, 2 * HEAD)
        kept[pl.ds(i * PAIR, PAIR), :] = part.astype(BF)
    scale = np.float32(1.0 / np.sqrt(HEAD))
    for i in range(RNG // 2):
        rows = pl.ds(i * PAIR, PAIR)
        window = pl.ds(i * PAIR, WINDOW)
        key = key_token[:, i * PAIR : i * PAIR + WINDOW]
        seen = (key >= start[rows, :]) & (key <= token[rows, :])
        bias[...] = jnp.where(seen, 0.0, -jnp.inf)
        scores[...] = lax.dot_general(
            q[i], kept[window, :HEAD], (((1,), (1,)), ((), ())), preferred_element_type=F32
        )
        for h in range(HEADS):
            head = pl.ds(h * PAIR, PAIR)
            s = scores[head, :] * scale + bias[...]
            weights = jnp.exp(s - jnp.max(s, axis=1, keepdims=True))
            total = jnp.sum(weights, axis=1, keepdims=True)
            probs[head, :] = (weights * (1.0 / total)).astype(BF)
        m = jnp.dot(probs[...], kept[window, HEAD:], preferred_element_type=F32)
        for h in range(HEADS):
            for r in range(2):
                mixed[h, pl.ds(2 * i + r, NF, stride=RNG), :] = m[h * PAIR + r * NF :][:NF]
    for h in range(HEADS):
        out[:, pl.ds(h * HEAD, HEAD)] = mixed[h].astype(BF)


def per_device(
    hidden_rows,
    queries,
    norm_gain,
    query_gain,
    key_norm_gain,
    key_matrix,
    value_matrix,
    lengths,
    owner,
):
    x, z, c = (lax.axis_index(a).astype(jnp.int32) for a in ("x", "z", "core"))
    zc = z * NC + c
    place = jnp.stack([x, z, c])
    fsdp = ("x", "z", "core")

    vmem = pl.BlockSpec(memory_space=pltpu.VMEM)
    smem = pl.BlockSpec(memory_space=pltpu.SMEM)
    packed = pl.pallas_call(
        pack_kernel,
        in_specs=[smem, vmem, vmem],
        out_specs=[vmem] * NX,
        out_shape=[jax.ShapeDtypeStruct((SHARD, 2 * HEAD), BF)] * NX,
        name="pack_weights",
    )(place, key_matrix, value_matrix)
    piece = jnp.stack(
        [packed[0]] + [shift(packed[k], "x", NX, -X_ORDER[k]) for k in range(1, NX)]
    )

    cut = ROWS // 2
    own_a, own_b = pl.pallas_call(
        norm_kernel,
        in_specs=[vmem, vmem],
        out_specs=[vmem] * 2,
        out_shape=[jax.ShapeDtypeStruct((cut, WIDTH), BF)] * 2,
        name="norm_hidden",
    )(hidden_rows, norm_gain.reshape(1, WIDTH))
    left_a = shift(own_a, "x", NX, 1)
    right_b = shift(own_b, "x", NX, -1)
    left_b = shift(own_b, "x", NX, 1)
    right_a = shift(own_a, "x", NX, -1)

    pieces = [piece]
    up = down = piece
    for step in range(NZ // 2 - 1):
        up = shift(up, "z", NZ, 1)
        down = shift(down, "z", NZ, -1)
        if step == 0:
            up, down, left_a, right_b = lax.optimization_barrier((up, down, left_a, right_b))
            far_a = shift(left_a, "x", NX, 1)
            far_b = shift(right_b, "x", NX, -1)
        pieces += [up, down]
    half = NX // 2
    last_a = shift(up[:half], "z", NZ, 1)
    last_b = shift(down[half:], "z", NZ, -1)
    pieces.append(jnp.concatenate([last_a, last_b], axis=0))
    mine, mine2 = jnp.stack(pieces[:NEAR]), jnp.stack(pieces[NEAR:])
    other, other2 = shift(mine, "core", NC, 1), shift(mine2, "core", NC, 1)

    sent = queries.reshape(NZ * NC, RNG, NX, HEADS * HEAD).transpose(2, 0, 1, 3)
    sent = sent.reshape(NF, RNG, HEADS * HEAD)
    got = lax.all_to_all(sent, fsdp, split_axis=0, concat_axis=0, tiled=True)

    rows = jnp.arange(ROWS, dtype=jnp.int32)
    chunk_x = jnp.stack([(x + by + NX) % NX for by in X_ORDER])
    made = (rows[None, :] * NF + chunk_x[:, None] * (NZ * NC) + zc).reshape(-1)
    key_cos, key_sin = rope_tables(made - rollout_starts(lengths, owner, made))
    token = zc * QTOK + jnp.arange(QTOK, dtype=jnp.int32)
    start = rollout_starts(lengths, owner, token)
    q_cos, q_sin = rope_tables(token - start)
    pair_rows = zc * RNG - HALO + jnp.arange(KROWS, dtype=jnp.int32).reshape(KROWS // 2, 1, 2, 1)
    key_token = (
        pair_rows * NF
        + chunk_x[None, None, None, :] * (NZ * NC)
        + jnp.arange(NZ * NC, dtype=jnp.int32)[None, :, None, None]
    ).reshape(1, KTOK)

    ready = pl.pallas_call(
        prepare_kernel,
        in_specs=[vmem] * 4,
        out_specs=vmem,
        out_shape=jax.ShapeDtypeStruct((RNG // 2, HEADS * PAIR, HEAD), BF),
        scratch_shapes=[pltpu.VMEM((HEADS, QTOK, HEAD), F32)],
        compiler_params=pltpu.CompilerParams(vmem_limit_bytes=32 * 2**20),
        name="prepare_queries",
    )(got.reshape(QTOK, HEADS * HEAD), query_gain.reshape(1, HEAD), q_cos, q_sin)

    anywhere = pl.BlockSpec(memory_space=pl.ANY)
    key_gain = key_norm_gain.reshape(1, HEAD)
    made_first, weight = pl.pallas_call(
        first_kernel,
        in_specs=[smem]
        + [vmem] * 6
        + [anywhere] * 4
        + [vmem] * 3,
        out_specs=[vmem] * 2,
        out_shape=[
            jax.ShapeDtypeStruct((NX - 1, 2, ROWS, HEAD), F32),
            jax.ShapeDtypeStruct((NX, NZ, NC, SHARD, 2 * HEAD), BF),
        ],
        scratch_shapes=[pltpu.SemaphoreType.DMA((2 * NZ * NX,))],
        compiler_params=pltpu.CompilerParams(vmem_limit_bytes=32 * 2**20),
        name="project_first",
    )(
        place,
        own_a,
        own_b,
        left_a,
        left_b,
        right_a,
        right_b,
        mine,
        mine2,
        other,
        other2,
        key_gain,
        key_cos,
        key_sin,
    )
    made_kv = pl.pallas_call(
        second_kernel,
        in_specs=[vmem] * 7,
        out_specs=vmem,
        out_shape=jax.ShapeDtypeStruct((NZ * NC, NX * KROWS, 2 * HEAD), BF),
        scratch_shapes=[pltpu.VMEM((NX * ROWS, HEAD), F32)] * 2,
        compiler_params=pltpu.CompilerParams(vmem_limit_bytes=32 * 2**20),
        name="project_last",
    )(far_a, far_b, weight, made_first, key_gain, key_cos, key_sin)
    kv = lax.all_to_all(made_kv, ("z", "core"), split_axis=0, concat_axis=0, tiled=True)

    mixed = pl.pallas_call(
        attend_kernel,
        in_specs=[vmem] * 5,
        out_specs=vmem,
        out_shape=jax.ShapeDtypeStruct((QTOK, HEADS * HEAD), BF),
        scratch_shapes=[
            pltpu.VMEM((PAIR, WINDOW), F32),
            pltpu.VMEM((KTOK, 2 * HEAD), BF),
            pltpu.VMEM((HEADS, QTOK, HEAD), F32),
            pltpu.VMEM((HEADS * PAIR, WINDOW), BF),
            pltpu.VMEM((HEADS * PAIR, WINDOW), F32),
        ],
        compiler_params=pltpu.CompilerParams(vmem_limit_bytes=32 * 2**20),
        name="attend",
    )(ready, kv, token[:, None], start[:, None], key_token)

    back = lax.all_to_all(
        mixed.reshape(NF, RNG, HEADS * HEAD), fsdp, split_axis=0, concat_axis=0, tiled=True
    )
    back = back.reshape(NX, NZ * NC, RNG, HEADS * HEAD).transpose(1, 2, 0, 3)
    return back.reshape(ROWS, NX * HEADS * HEAD)


def solution(mesh):
    grid = Mesh(mesh.devices.reshape(NX, NZ, NC, mesh.devices.shape[1]), ("x", "z", "core", "rep"))
    fsdp = ("x", "z", "core")
    whole = P(("rep",) + fsdp, None)
    placed = (whole, whole, P(), P(), P(), P(fsdp, None), P(fsdp, None), P("rep"), P("rep"))
    return jax.shard_map(
        per_device, mesh=grid, in_specs=placed, out_specs=whole, check_vma=False
    )
```

```python
import functools

import jax
import jax.numpy as jnp
import numpy as np
from jax import lax
from jax.experimental import pallas as pl
from jax.experimental.pallas import tpu as pltpu
from jax.sharding import Mesh, PartitionSpec as P

NX, NZ, NC = 4, 8, 2
NF = NX * NZ * NC
WIDTH = 5120
HEADS = 8
HEAD = 128
ROWS = 128
SHARD = WIDTH // NF
BLOCK = 8
HALO = 4
BLOCKS = ROWS // BLOCK
KTOK = NF * (BLOCK + HALO)
QTOK = NX * BLOCK
PAD = NX * HALO
X_ORDER = (0, -1, 1, 2)
Z_ORDER = (0, -1, 1, -2, 2, -3, 3, 4)
NEAR = 5

eps = 1e-06
rope_base = 1000000.0
BF = jnp.bfloat16
F32 = jnp.float32


def shift(value, axis, size, by):
    return lax.ppermute(value, axis, [(i, (i + by) % size) for i in range(size)])


def rollout_starts(lengths, owner, tokens):
    index = jnp.arange(lengths.shape[0], dtype=jnp.int32)
    earlier = (owner[None, :] < owner[:, None]) | (owner[None, :] == owner[:, None]) & (
        index[None, :] < index[:, None]
    )
    offset = jnp.sum(jnp.where(earlier, lengths[None, :], 0), axis=1)
    return jnp.max(jnp.where(offset[None, :] <= tokens[:, None], offset[None, :], 0), axis=1)


def rope_tables(positions):
    half = HEAD // 2
    steps = jnp.arange(half, dtype=F32) * (2.0 / HEAD)
    inverse = jnp.power(F32(rope_base), -steps)
    angles = positions.astype(F32)[:, None] * inverse[None, :]
    cosine = jnp.cos(angles)
    sine = jnp.sin(angles)
    return (
        jnp.concatenate([cosine, cosine], axis=1),
        jnp.concatenate([-sine, sine], axis=1),
    )


def normed_rope(value, gain, cosine, sine):
    mean_square = jnp.mean(value * value, axis=-1, keepdims=True)
    value = value * lax.rsqrt(mean_square + eps) * gain
    return value * cosine + pltpu.roll(value, HEAD // 2, 1) * sine


def pack_kernel(place, key, value, *out):
    for k, by in enumerate(X_ORDER):
        head = lax.rem(place[0] - by + NX, NX)
        lanes = pl.ds(pl.multiple_of(head * HEAD, HEAD), HEAD)
        out[k][:, :HEAD] = key[:, lanes]
        out[k][:, HEAD:] = value[:, lanes]


def stack_kernel(place, *refs):
    for k, by in enumerate(X_ORDER):
        refs[-1][lax.rem(place[0] + by + NX, NX)] = refs[k][...]


def norm_kernel(hidden, gain, out):
    block = 16
    for i in range(0, ROWS, block):
        value = hidden[i : i + block, :].astype(F32)
        mean_square = jnp.mean(value * value, axis=-1, keepdims=True)
        value = value * lax.rsqrt(mean_square + eps) * gain[...]
        out[i : i + block, :] = value.astype(BF)


def project(x, w, gain, cosine, sine):
    raw = jnp.dot(x, w, preferred_element_type=F32)
    return normed_rope(raw[:, :HEAD], gain, cosine, sine), raw[:, HEAD:]


def first_kernel(
    place,
    own,
    left,
    right,
    mine,
    mine2,
    other,
    other2,
    gain,
    cosine,
    sine,
    out,
    weight,
    tokens,
    sem,
    token_sem,
):
    z, c = place[1], place[2]
    copies = []
    for k, by in enumerate(Z_ORDER):
        at = lax.rem(z + by + NZ, NZ)
        near = k < NEAR
        for which, core in (((mine, mine2)[k >= NEAR], c), ((other, other2)[k >= NEAR], 1 - c)):
            copies.append(
                pltpu.make_async_copy(
                    which.at[k if near else k - NEAR], weight.at[:, at, core], sem.at[len(copies)]
                )
            )
    loads = []
    for k, chunk in enumerate((own, left, right)):
        loads.append(pltpu.make_async_copy(chunk, tokens.at[k], token_sem.at[k]))
    for copy in copies + loads:
        copy.start()
    for copy in copies:
        copy.wait()
    w = weight[...].reshape(WIDTH, 2 * HEAD)
    for k, load in enumerate(loads):
        load.wait()
        rows = pl.ds(k * ROWS, ROWS)
        key, value = project(tokens[k], w, gain[...], cosine[rows, :], sine[rows, :])
        out[k, 0] = key
        out[k, 1] = value


def second_kernel(far_a, far_b, weight, made, gain, cosine, sine, out, keep_k, keep_v):
    w = weight[...].reshape(WIDTH, 2 * HEAD)
    x = jnp.concatenate([far_a[...], far_b[...]], axis=0)
    rows = pl.ds((NX - 1) * ROWS, ROWS)
    far = project(x, w, gain[...], cosine[rows, :], sine[rows, :])
    for side, keep in enumerate((keep_k, keep_v)):
        for k in range(NX - 1):
            keep[pl.ds(k, ROWS, stride=NX), :] = made[k, side]
        keep[pl.ds(NX - 1, ROWS, stride=NX), :] = far[side]
        out[:, pl.ds(side * HEAD, HEAD)] = keep[...].astype(BF)


def split_kernel(place, q, *out):
    width = HEADS * HEAD
    for k, by in enumerate(X_ORDER):
        x = lax.rem(place[0] - by + NX, NX)
        out[k][...] = q[:, pl.ds(pl.multiple_of(x * width, width), width)]


def join_kernel(place, *refs):
    out = refs[-1]
    width = HEADS * HEAD
    for k, by in enumerate(X_ORDER):
        x = lax.rem(place[0] - by + NX, NX)
        out[:, pl.ds(pl.multiple_of(x * width, width), width)] = refs[k][...]


def prepare_kernel(q0, q1, q2, q3, gain, cosine, sine, out):
    for h in range(HEADS):
        lanes = pl.ds(h * HEAD, HEAD)
        done = []
        for k, q in enumerate((q0, q1, q2, q3)):
            rows = pl.ds(k * ROWS, ROWS)
            value = q[:, lanes].astype(F32)
            done.append(normed_rope(value, gain[...], cosine[rows, :], sine[rows, :]))
        for b in range(BLOCKS):
            rows = slice(b * BLOCK, (b + 1) * BLOCK)
            block = jnp.concatenate([value[rows] for value in done], axis=0)
            out[b, pl.ds(h * QTOK, QTOK), :] = block.astype(BF)


def attend_kernel(
    place,
    q_in,
    mine,
    mine2,
    mine3,
    other,
    other2,
    other3,
    token_in,
    start_in,
    key_token,
    o0,
    o1,
    o2,
    o3,
    kv,
    q,
    token,
    start,
    probs,
    scores,
    mixed,
    sem,
):
    copies = [
        pltpu.make_async_copy(q_in, q, sem.at[0]),
        pltpu.make_async_copy(token_in, token, sem.at[1]),
        pltpu.make_async_copy(start_in, start, sem.at[2]),
    ]
    for side, group in enumerate(((mine, mine2, mine3), (other, other2, other3))):
        at = 0
        for part in group:
            count = part.shape[0]
            copies.append(
                pltpu.make_async_copy(
                    part,
                    kv.at[side, pl.ds(at, count), pl.ds(PAD, NX * ROWS), :],
                    sem.at[len(copies)],
                )
            )
            at += count
    for copy in copies:
        copy.start()
    kv[:, :, :PAD, :] = jnp.zeros((NC, NZ, PAD, 2 * HEAD), BF)
    for copy in copies:
        copy.wait()
    scale = np.float32(1.0 / np.sqrt(HEAD))

    def window(b, side):
        rows = pl.ds(b * QTOK, PAD + QTOK)
        return kv[:, :, rows, pl.ds(side * HEAD, HEAD)].reshape(KTOK, HEAD)

    def score(b):
        scores[b % 2] = lax.dot_general(
            q[b], window(b, 0), (((1,), (1,)), ((), ())), preferred_element_type=F32
        )

    score(0)
    for b in range(BLOCKS):
        slot = b % 2
        if b + 1 < BLOCKS:
            score(b + 1)
        key = key_token[...] + b * BLOCK * NF
        seen = (key >= start[b]) & (key <= token[b])
        bias = jnp.where(seen, 0.0, -jnp.inf)
        for h in range(HEADS):
            head = pl.ds(h * QTOK, QTOK)
            s = scores[slot, head, :] * scale + bias
            weights = jnp.exp(s - jnp.max(s, axis=1, keepdims=True))
            total = jnp.sum(weights, axis=1, keepdims=True)
            probs[slot, head, :] = (weights * (1.0 / total)).astype(BF)
        m = jnp.dot(probs[slot], window(b, 1), preferred_element_type=F32)
        for h in range(HEADS):
            for k in range(NX):
                at = h * QTOK + k * BLOCK
                mixed[k, pl.ds(b * BLOCK, BLOCK), pl.ds(h * HEAD, HEAD)] = m[at : at + BLOCK]
    for k, out in enumerate((o0, o1, o2, o3)):
        out[...] = mixed[k].astype(BF)


def per_device(
    hidden_rows,
    queries,
    norm_gain,
    query_gain,
    key_norm_gain,
    key_matrix,
    value_matrix,
    lengths,
    owner,
):
    x, z, c = (lax.axis_index(a).astype(jnp.int32) for a in ("x", "z", "core"))
    zc = z * NC + c
    place = jnp.stack([x, z, c])
    vmem = pl.BlockSpec(memory_space=pltpu.VMEM)
    anywhere = pl.BlockSpec(memory_space=pl.ANY)
    smem = pl.BlockSpec(memory_space=pltpu.SMEM)
    rows = jnp.arange(ROWS, dtype=jnp.int32)
    chunk_x = jnp.stack([(x + by + NX) % NX for by in X_ORDER])
    token = rows[None, :] * NF + chunk_x[:, None] * (NZ * NC) + zc
    start = rollout_starts(lengths, owner, token.reshape(-1))
    key_cos, key_sin = rope_tables(token.reshape(-1) - start)

    def blocked(value):
        value = value.reshape(NX, BLOCKS, BLOCK).transpose(1, 0, 2)
        return value.reshape(BLOCKS, QTOK, 1)

    core = jnp.stack([c, 1 - c])
    around = jnp.stack([(z + by + NZ) % NZ for by in Z_ORDER])
    key_rows = jnp.arange(-HALO, BLOCK, dtype=jnp.int32)
    key_token = (
        key_rows[None, None, :, None] * NF
        + chunk_x[None, None, None, :] * (NZ * NC)
        + around[None, :, None, None] * NC
        + core[:, None, None, None]
    ).reshape(1, KTOK)

    seen_by = (blocked(token), blocked(start), key_token)

    bar = lax.optimization_barrier
    packed = pl.pallas_call(
        pack_kernel,
        in_specs=[smem, vmem, vmem],
        out_specs=[vmem] * NX,
        out_shape=[jax.ShapeDtypeStruct((SHARD, 2 * HEAD), BF)] * NX,
        name="pack_weights",
    )(place, key_matrix, value_matrix)
    hidden_rows, packed = bar((hidden_rows, packed))
    own = pl.pallas_call(
        norm_kernel,
        in_specs=[vmem, vmem],
        out_specs=vmem,
        out_shape=jax.ShapeDtypeStruct((ROWS, WIDTH), BF),
        name="norm_hidden",
    )(hidden_rows, norm_gain.reshape(1, WIDTH))
    piece = pl.pallas_call(
        stack_kernel,
        in_specs=[smem] + [vmem] * NX,
        out_specs=vmem,
        out_shape=jax.ShapeDtypeStruct((NX, SHARD, 2 * HEAD), BF),
        name="stack_weights",
    )(place, packed[0], *[shift(packed[k], "x", NX, -X_ORDER[k]) for k in range(1, NX)])

    parts = pl.pallas_call(
        split_kernel,
        in_specs=[smem, vmem],
        out_specs=[vmem] * NX,
        out_shape=[jax.ShapeDtypeStruct((ROWS, HEADS * HEAD), BF)] * NX,
        name="split_queries",
    )(place, queries)
    piece, own = bar((piece, own))
    left = shift(own, "x", NX, 1)
    right = shift(own, "x", NX, -1)

    cut = ROWS // 2
    pieces = [piece]
    up = down = piece
    for step in range(NZ // 2 - 1):
        up = shift(up, "z", NZ, 1)
        down = shift(down, "z", NZ, -1)
        if step == 0:
            up, down, seen_by, key_cos, key_sin, parts = bar(
                (up, down, seen_by, key_cos, key_sin, parts)
            )
        if step == 2:
            up, down, left, right = bar((up, down, left, right))
            far_a = shift(left[:cut], "x", NX, 1)
            far_b = shift(right[cut:], "x", NX, -1)
        pieces += [up, down]
    half = NX // 2
    last_a = shift(up[:half], "z", NZ, 1)
    last_b = shift(down[half:], "z", NZ, -1)
    pieces.append(jnp.concatenate([last_a, last_b], axis=0))
    mine, mine2 = jnp.stack(pieces[:NEAR]), jnp.stack(pieces[NEAR:])
    mine2, far_a, far_b = bar((mine2, far_a, far_b))
    other, other2 = shift(mine, "core", NC, 1), shift(mine2, "core", NC, 1)

    parts, far_a, far_b = bar((parts, far_a, far_b))
    got = [parts[0]] + [shift(parts[k], "x", NX, -X_ORDER[k]) for k in range(1, NX)]

    key_gain = key_norm_gain.reshape(1, HEAD)
    made_first, weight = pl.pallas_call(
        first_kernel,
        in_specs=[smem] + [anywhere] * 7 + [vmem] * 3,
        out_specs=[vmem] * 2,
        out_shape=[
            jax.ShapeDtypeStruct((NX - 1, 2, ROWS, HEAD), F32),
            jax.ShapeDtypeStruct((NX, NZ, NC, SHARD, 2 * HEAD), BF),
        ],
        scratch_shapes=[
            pltpu.VMEM((NX - 1, ROWS, WIDTH), BF),
            pltpu.SemaphoreType.DMA((2 * NZ,)),
            pltpu.SemaphoreType.DMA((NX - 1,)),
        ],
        compiler_params=pltpu.CompilerParams(vmem_limit_bytes=32 * 2**20),
        name="project_first",
    )(place, own, left, right, mine, mine2, other, other2, key_gain, key_cos, key_sin)
    made_kv = pl.pallas_call(
        second_kernel,
        in_specs=[vmem] * 7,
        out_specs=vmem,
        out_shape=jax.ShapeDtypeStruct((NX * ROWS, 2 * HEAD), BF),
        scratch_shapes=[pltpu.VMEM((NX * ROWS, HEAD), F32)] * 2,
        compiler_params=pltpu.CompilerParams(vmem_limit_bytes=32 * 2**20),
        name="project_last",
    )(far_a, far_b, weight, made_first, key_gain, key_cos, key_sin)
    def prepare(got):
        return pl.pallas_call(
            prepare_kernel,
            in_specs=[vmem] * 7,
            out_specs=vmem,
            out_shape=jax.ShapeDtypeStruct((BLOCKS, HEADS * QTOK, HEAD), BF),
            compiler_params=pltpu.CompilerParams(vmem_limit_bytes=32 * 2**20),
            name="prepare_queries",
        )(*got, query_gain.reshape(1, HEAD), key_cos, key_sin)

    up = down = made_kv
    first, second = [made_kv], []
    for step in range(NZ // 2 - 1):
        up = shift(up, "z", NZ, 1)
        down = shift(down, "z", NZ, -1)
        if step == 0:
            up, down, got = bar((up, down, got))
            ready = prepare(got)
        if step == 2:
            up, down, ready = bar((up, down, ready))
        (first if step < 2 else second).extend([up, down])
    half = NX * ROWS // 2
    third = jnp.concatenate(
        [shift(up[:half], "z", NZ, 1), shift(down[half:], "z", NZ, -1)], axis=0
    )
    groups = [jnp.stack(first), jnp.stack(second), third[None]]
    crossed = [shift(group, "core", NC, 1) for group in groups]

    mixed = pl.pallas_call(
        attend_kernel,
        in_specs=[smem] + [anywhere] * 9 + [vmem],
        out_specs=[vmem] * NX,
        out_shape=[jax.ShapeDtypeStruct((ROWS, HEADS * HEAD), BF)] * NX,
        scratch_shapes=[
            pltpu.VMEM((NC, NZ, PAD + NX * ROWS, 2 * HEAD), BF),
            pltpu.VMEM((BLOCKS, HEADS * QTOK, HEAD), BF),
            pltpu.VMEM((BLOCKS, QTOK, 1), jnp.int32),
            pltpu.VMEM((BLOCKS, QTOK, 1), jnp.int32),
            pltpu.VMEM((2, HEADS * QTOK, KTOK), BF),
            pltpu.VMEM((2, HEADS * QTOK, KTOK), F32),
            pltpu.VMEM((NX, ROWS, HEADS * HEAD), F32),
            pltpu.SemaphoreType.DMA((9,)),
        ],
        compiler_params=pltpu.CompilerParams(vmem_limit_bytes=40 * 2**20),
        name="attend",
    )(place, ready, *groups, *crossed, *seen_by)
    back = [mixed[0]] + [shift(mixed[k], "x", NX, X_ORDER[k]) for k in range(1, NX)]
    return pl.pallas_call(
        join_kernel,
        in_specs=[smem] + [vmem] * NX,
        out_specs=vmem,
        out_shape=jax.ShapeDtypeStruct((ROWS, NX * HEADS * HEAD), BF),
        name="join_heads",
    )(place, *back)


def solution(mesh):
    grid = Mesh(mesh.devices.reshape(NX, NZ, NC, mesh.devices.shape[1]), ("x", "z", "core", "rep"))
    fsdp = ("x", "z", "core")
    whole = P(("rep",) + fsdp, None)
    placed = (whole, whole, P(), P(), P(), P(fsdp, None), P(fsdp, None), P("rep"), P("rep"))
    return jax.shard_map(
        per_device, mesh=grid, in_specs=placed, out_specs=whole, check_vma=False
    )
```

```python
import functools

import jax
import jax.numpy as jnp
import numpy as np
from jax import lax
from jax.experimental import pallas as pl
from jax.experimental.pallas import tpu as pltpu
from jax.sharding import Mesh, PartitionSpec as P

NX, NZ, NC = 4, 8, 2
NF = NX * NZ * NC
WIDTH = 5120
HEADS = 8
HEAD = 128
ROWS = 128
SHARD = WIDTH // NF
BLOCK = 8
HALO = 4
BLOCKS = ROWS // BLOCK
KTOK = NF * (BLOCK + HALO)
QTOK = NX * BLOCK
PAD = NX * HALO
X_ORDER = (0, -1, 1, 2)
Z_ORDER = (0, -1, 1, -2, 2, -3, 3, 4)
NEAR = 5

eps = 1e-06
rope_base = 1000000.0
BF = jnp.bfloat16
F32 = jnp.float32


def shift(value, axis, size, by):
    return lax.ppermute(value, axis, [(i, (i + by) % size) for i in range(size)])


def rollout_starts(lengths, owner, tokens):
    index = jnp.arange(lengths.shape[0], dtype=jnp.int32)
    earlier = (owner[None, :] < owner[:, None]) | (owner[None, :] == owner[:, None]) & (
        index[None, :] < index[:, None]
    )
    offset = jnp.sum(jnp.where(earlier, lengths[None, :], 0), axis=1)
    return jnp.max(jnp.where(offset[None, :] <= tokens[:, None], offset[None, :], 0), axis=1)


def rope_tables(positions):
    half = HEAD // 2
    steps = jnp.arange(half, dtype=F32) * (2.0 / HEAD)
    inverse = jnp.power(F32(rope_base), -steps)
    angles = positions.astype(F32)[:, None] * inverse[None, :]
    cosine = jnp.cos(angles)
    sine = jnp.sin(angles)
    return (
        jnp.concatenate([cosine, cosine], axis=1),
        jnp.concatenate([-sine, sine], axis=1),
    )


def normed_rope(value, gain, cosine, sine):
    mean_square = jnp.mean(value * value, axis=-1, keepdims=True)
    value = value * lax.rsqrt(mean_square + eps) * gain
    return value * cosine + pltpu.roll(value, HEAD // 2, 1) * sine


def pack_kernel(place, key, value, *out):
    for k, by in enumerate(X_ORDER):
        head = lax.rem(place[0] - by + NX, NX)
        lanes = pl.ds(pl.multiple_of(head * HEAD, HEAD), HEAD)
        out[k][:, :HEAD] = key[:, lanes]
        out[k][:, HEAD:] = value[:, lanes]


def stack_kernel(place, *refs):
    for k, by in enumerate(X_ORDER):
        refs[-1][lax.rem(place[0] + by + NX, NX)] = refs[k][...]


def norm_kernel(hidden, gain, out):
    block = 16

    def body(i, carry):
        rows = pl.ds(pl.multiple_of(i * block, block), block)
        value = hidden[rows, :].astype(F32)
        mean_square = jnp.mean(value * value, axis=-1, keepdims=True)
        value = value * lax.rsqrt(mean_square + eps) * gain[...]
        out[rows, :] = value.astype(BF)
        return carry

    lax.fori_loop(0, ROWS // block, body, 0)


def project(x, w, gain, cosine, sine):
    raw = jnp.dot(x, w, preferred_element_type=F32)
    return normed_rope(raw[:, :HEAD], gain, cosine, sine), raw[:, HEAD:]


def first_kernel(
    place,
    own,
    left,
    right,
    mine,
    mine2,
    other,
    other2,
    gain,
    cosine,
    sine,
    out,
    weight,
    tokens,
    sem,
    token_sem,
):
    z, c = place[1], place[2]
    copies = []
    for k, by in enumerate(Z_ORDER):
        at = lax.rem(z + by + NZ, NZ)
        near = k < NEAR
        for which, core in (((mine, mine2)[k >= NEAR], c), ((other, other2)[k >= NEAR], 1 - c)):
            copies.append(
                pltpu.make_async_copy(
                    which.at[k if near else k - NEAR], weight.at[:, at, core], sem.at[len(copies)]
                )
            )
    loads = []
    for k, chunk in enumerate((own, left, right)):
        loads.append(pltpu.make_async_copy(chunk, tokens.at[k], token_sem.at[k]))
    for copy in copies + loads:
        copy.start()
    for copy in copies:
        copy.wait()
    w = weight[...].reshape(WIDTH, 2 * HEAD)
    for load in loads:
        load.wait()

    def body(k, carry):
        rows = pl.ds(pl.multiple_of(k * ROWS, ROWS), ROWS)
        key, value = project(tokens[k], w, gain[...], cosine[rows, :], sine[rows, :])
        out[k, 0] = key
        out[k, 1] = value
        return carry

    lax.fori_loop(0, NX - 1, body, 0)


def second_kernel(far_a, far_b, weight, made, gain, cosine, sine, out, keep_k, keep_v):
    w = weight[...].reshape(WIDTH, 2 * HEAD)
    x = jnp.concatenate([far_a[...], far_b[...]], axis=0)
    rows = pl.ds((NX - 1) * ROWS, ROWS)
    far = project(x, w, gain[...], cosine[rows, :], sine[rows, :])
    for side, keep in enumerate((keep_k, keep_v)):
        for k in range(NX - 1):
            keep[pl.ds(k, ROWS, stride=NX), :] = made[k, side]
        keep[pl.ds(NX - 1, ROWS, stride=NX), :] = far[side]
        out[:, pl.ds(side * HEAD, HEAD)] = keep[...].astype(BF)


def split_kernel(place, q, *out):
    width = HEADS * HEAD
    for k, by in enumerate(X_ORDER):
        x = lax.rem(place[0] - by + NX, NX)
        out[k][...] = q[:, pl.ds(pl.multiple_of(x * width, width), width)]


def join_kernel(place, *refs):
    out = refs[-1]
    width = HEADS * HEAD
    for k, by in enumerate(X_ORDER):
        x = lax.rem(place[0] - by + NX, NX)
        out[:, pl.ds(pl.multiple_of(x * width, width), width)] = refs[k][...]


def prepare_kernel(q0, q1, q2, q3, gain, cosine, sine, out):
    def body(h, carry):
        lanes = pl.ds(pl.multiple_of(h * HEAD, HEAD), HEAD)
        done = []
        for k, q in enumerate((q0, q1, q2, q3)):
            rows = pl.ds(k * ROWS, ROWS)
            value = q[:, lanes].astype(F32)
            done.append(normed_rope(value, gain[...], cosine[rows, :], sine[rows, :]))
        for b in range(BLOCKS):
            rows = slice(b * BLOCK, (b + 1) * BLOCK)
            block = jnp.concatenate([value[rows] for value in done], axis=0)
            at = pl.ds(pl.multiple_of(h * QTOK, QTOK), QTOK)
            out[b, at, :] = block.astype(BF)
        return carry

    lax.fori_loop(0, HEADS, body, 0)


def attend_kernel(
    place,
    q_in,
    mine,
    mine2,
    mine3,
    other,
    other2,
    other3,
    token_in,
    start_in,
    key_token,
    o0,
    o1,
    o2,
    o3,
    kv,
    q,
    token,
    start,
    probs,
    scores,
    mixed,
    sem,
):
    copies = [
        pltpu.make_async_copy(q_in, q, sem.at[0]),
        pltpu.make_async_copy(token_in, token, sem.at[1]),
        pltpu.make_async_copy(start_in, start, sem.at[2]),
    ]
    for side, group in enumerate(((mine, mine2, mine3), (other, other2, other3))):
        at = 0
        for part in group:
            count = part.shape[0]
            copies.append(
                pltpu.make_async_copy(
                    part,
                    kv.at[side, pl.ds(at, count), pl.ds(PAD, NX * ROWS), :],
                    sem.at[len(copies)],
                )
            )
            at += count
    for copy in copies:
        copy.start()
    kv[:, :, :PAD, :] = jnp.zeros((NC, NZ, PAD, 2 * HEAD), BF)
    for copy in copies:
        copy.wait()
    scale = np.float32(1.0 / np.sqrt(HEAD))

    def window(b, side):
        rows = pl.ds(pl.multiple_of(b * QTOK, QTOK), PAD + QTOK)
        return kv[:, :, rows, pl.ds(side * HEAD, HEAD)].reshape(KTOK, HEAD)

    def score(b, slot):
        scores[slot] = lax.dot_general(
            q[b], window(b, 0), (((1,), (1,)), ((), ())), preferred_element_type=F32
        )

    score(0, 0)

    def body(i, carry):
        for slot in range(2):
            b = 2 * i + slot
            score(jnp.minimum(b + 1, BLOCKS - 1), 1 - slot)
            key = key_token[...] + b * BLOCK * NF
            seen = (key >= start[b]) & (key <= token[b])
            bias = jnp.where(seen, 0.0, -jnp.inf)
            for h in range(HEADS):
                head = pl.ds(h * QTOK, QTOK)
                s = scores[slot, head, :] * scale + bias
                weights = jnp.exp(s - jnp.max(s, axis=1, keepdims=True))
                total = jnp.sum(weights, axis=1, keepdims=True)
                probs[slot, head, :] = (weights * (1.0 / total)).astype(BF)
            m = jnp.dot(probs[slot], window(b, 1), preferred_element_type=F32)
            rows = pl.ds(pl.multiple_of(b * BLOCK, BLOCK), BLOCK)
            for h in range(HEADS):
                for k in range(NX):
                    at = h * QTOK + k * BLOCK
                    mixed[k, rows, pl.ds(h * HEAD, HEAD)] = m[at : at + BLOCK]
        return carry

    lax.fori_loop(0, BLOCKS // 2, body, 0)
    for k, out in enumerate((o0, o1, o2, o3)):
        out[...] = mixed[k].astype(BF)


def per_device(
    hidden_rows,
    queries,
    norm_gain,
    query_gain,
    key_norm_gain,
    key_matrix,
    value_matrix,
    lengths,
    owner,
):
    x, z, c = (lax.axis_index(a).astype(jnp.int32) for a in ("x", "z", "core"))
    zc = z * NC + c
    place = jnp.stack([x, z, c])
    vmem = pl.BlockSpec(memory_space=pltpu.VMEM)
    anywhere = pl.BlockSpec(memory_space=pl.ANY)
    smem = pl.BlockSpec(memory_space=pltpu.SMEM)
    rows = jnp.arange(ROWS, dtype=jnp.int32)
    chunk_x = jnp.stack([(x + by + NX) % NX for by in X_ORDER])
    token = rows[None, :] * NF + chunk_x[:, None] * (NZ * NC) + zc
    start = rollout_starts(lengths, owner, token.reshape(-1))
    key_cos, key_sin = rope_tables(token.reshape(-1) - start)

    def blocked(value):
        value = value.reshape(NX, BLOCKS, BLOCK).transpose(1, 0, 2)
        return value.reshape(BLOCKS, QTOK, 1)

    core = jnp.stack([c, 1 - c])
    around = jnp.stack([(z + by + NZ) % NZ for by in Z_ORDER])
    key_rows = jnp.arange(-HALO, BLOCK, dtype=jnp.int32)
    key_token = (
        key_rows[None, None, :, None] * NF
        + chunk_x[None, None, None, :] * (NZ * NC)
        + around[None, :, None, None] * NC
        + core[:, None, None, None]
    ).reshape(1, KTOK)

    seen_by = (blocked(token), blocked(start), key_token)

    bar = lax.optimization_barrier
    packed = pl.pallas_call(
        pack_kernel,
        in_specs=[smem, vmem, vmem],
        out_specs=[vmem] * NX,
        out_shape=[jax.ShapeDtypeStruct((SHARD, 2 * HEAD), BF)] * NX,
        name="pack_weights",
    )(place, key_matrix, value_matrix)
    hidden_rows, packed = bar((hidden_rows, packed))
    own = pl.pallas_call(
        norm_kernel,
        in_specs=[vmem, vmem],
        out_specs=vmem,
        out_shape=jax.ShapeDtypeStruct((ROWS, WIDTH), BF),
        name="norm_hidden",
    )(hidden_rows, norm_gain.reshape(1, WIDTH))
    piece = pl.pallas_call(
        stack_kernel,
        in_specs=[smem] + [vmem] * NX,
        out_specs=vmem,
        out_shape=jax.ShapeDtypeStruct((NX, SHARD, 2 * HEAD), BF),
        name="stack_weights",
    )(place, packed[0], *[shift(packed[k], "x", NX, -X_ORDER[k]) for k in range(1, NX)])

    parts = pl.pallas_call(
        split_kernel,
        in_specs=[smem, vmem],
        out_specs=[vmem] * NX,
        out_shape=[jax.ShapeDtypeStruct((ROWS, HEADS * HEAD), BF)] * NX,
        name="split_queries",
    )(place, queries)
    piece, own = bar((piece, own))
    left = shift(own, "x", NX, 1)
    right = shift(own, "x", NX, -1)

    cut = ROWS // 2
    pieces = [piece]
    up = down = piece
    for step in range(NZ // 2 - 1):
        up = shift(up, "z", NZ, 1)
        down = shift(down, "z", NZ, -1)
        if step == 0:
            up, down, seen_by, key_cos, key_sin, parts = bar(
                (up, down, seen_by, key_cos, key_sin, parts)
            )
        if step == 2:
            up, down, left, right = bar((up, down, left, right))
            far_a = shift(left[:cut], "x", NX, 1)
            far_b = shift(right[cut:], "x", NX, -1)
        pieces += [up, down]
    half = NX // 2
    last_a = shift(up[:half], "z", NZ, 1)
    last_b = shift(down[half:], "z", NZ, -1)
    pieces.append(jnp.concatenate([last_a, last_b], axis=0))
    mine, mine2 = jnp.stack(pieces[:NEAR]), jnp.stack(pieces[NEAR:])
    mine2, far_a, far_b = bar((mine2, far_a, far_b))
    other, other2 = shift(mine, "core", NC, 1), shift(mine2, "core", NC, 1)

    parts, far_a, far_b = bar((parts, far_a, far_b))
    got = [parts[0]] + [shift(parts[k], "x", NX, -X_ORDER[k]) for k in range(1, NX)]

    key_gain = key_norm_gain.reshape(1, HEAD)
    made_first, weight = pl.pallas_call(
        first_kernel,
        in_specs=[smem] + [anywhere] * 7 + [vmem] * 3,
        out_specs=[vmem] * 2,
        out_shape=[
            jax.ShapeDtypeStruct((NX - 1, 2, ROWS, HEAD), F32),
            jax.ShapeDtypeStruct((NX, NZ, NC, SHARD, 2 * HEAD), BF),
        ],
        scratch_shapes=[
            pltpu.VMEM((NX - 1, ROWS, WIDTH), BF),
            pltpu.SemaphoreType.DMA((2 * NZ,)),
            pltpu.SemaphoreType.DMA((NX - 1,)),
        ],
        compiler_params=pltpu.CompilerParams(vmem_limit_bytes=32 * 2**20),
        name="project_first",
    )(place, own, left, right, mine, mine2, other, other2, key_gain, key_cos, key_sin)
    made_kv = pl.pallas_call(
        second_kernel,
        in_specs=[vmem] * 7,
        out_specs=vmem,
        out_shape=jax.ShapeDtypeStruct((NX * ROWS, 2 * HEAD), BF),
        scratch_shapes=[pltpu.VMEM((NX * ROWS, HEAD), F32)] * 2,
        compiler_params=pltpu.CompilerParams(vmem_limit_bytes=32 * 2**20),
        name="project_last",
    )(far_a, far_b, weight, made_first, key_gain, key_cos, key_sin)
    def prepare(got):
        return pl.pallas_call(
            prepare_kernel,
            in_specs=[vmem] * 7,
            out_specs=vmem,
            out_shape=jax.ShapeDtypeStruct((BLOCKS, HEADS * QTOK, HEAD), BF),
            compiler_params=pltpu.CompilerParams(vmem_limit_bytes=32 * 2**20),
            name="prepare_queries",
        )(*got, query_gain.reshape(1, HEAD), key_cos, key_sin)

    up = down = made_kv
    first, second = [made_kv], []
    for step in range(NZ // 2 - 1):
        up = shift(up, "z", NZ, 1)
        down = shift(down, "z", NZ, -1)
        if step == 0:
            up, down, got = bar((up, down, got))
            ready = prepare(got)
        if step == 2:
            up, down, ready = bar((up, down, ready))
        (first if step < 2 else second).extend([up, down])
    half = NX * ROWS // 2
    third = jnp.concatenate(
        [shift(up[:half], "z", NZ, 1), shift(down[half:], "z", NZ, -1)], axis=0
    )
    groups = [jnp.stack(first), jnp.stack(second), third[None]]
    crossed = [shift(group, "core", NC, 1) for group in groups]

    mixed = pl.pallas_call(
        attend_kernel,
        in_specs=[smem] + [anywhere] * 9 + [vmem],
        out_specs=[vmem] * NX,
        out_shape=[jax.ShapeDtypeStruct((ROWS, HEADS * HEAD), BF)] * NX,
        scratch_shapes=[
            pltpu.VMEM((NC, NZ, PAD + NX * ROWS, 2 * HEAD), BF),
            pltpu.VMEM((BLOCKS, HEADS * QTOK, HEAD), BF),
            pltpu.VMEM((BLOCKS, QTOK, 1), jnp.int32),
            pltpu.VMEM((BLOCKS, QTOK, 1), jnp.int32),
            pltpu.VMEM((2, HEADS * QTOK, KTOK), BF),
            pltpu.VMEM((2, HEADS * QTOK, KTOK), F32),
            pltpu.VMEM((NX, ROWS, HEADS * HEAD), F32),
            pltpu.SemaphoreType.DMA((9,)),
        ],
        compiler_params=pltpu.CompilerParams(vmem_limit_bytes=40 * 2**20),
        name="attend",
    )(place, ready, *groups, *crossed, *seen_by)
    back = [mixed[0]] + [shift(mixed[k], "x", NX, X_ORDER[k]) for k in range(1, NX)]
    return pl.pallas_call(
        join_kernel,
        in_specs=[smem] + [vmem] * NX,
        out_specs=vmem,
        out_shape=jax.ShapeDtypeStruct((ROWS, NX * HEADS * HEAD), BF),
        name="join_heads",
    )(place, *back)


def solution(mesh):
    grid = Mesh(mesh.devices.reshape(NX, NZ, NC, mesh.devices.shape[1]), ("x", "z", "core", "rep"))
    fsdp = ("x", "z", "core")
    whole = P(("rep",) + fsdp, None)
    placed = (whole, whole, P(), P(), P(), P(fsdp, None), P(fsdp, None), P("rep"), P("rep"))
    return jax.shard_map(
        per_device, mesh=grid, in_specs=placed, out_specs=whole, check_vma=False
    )
```

```python
import functools

import jax
import jax.numpy as jnp
import numpy as np
from jax import lax
from jax.experimental import pallas as pl
from jax.experimental.pallas import tpu as pltpu
from jax.sharding import Mesh, PartitionSpec as P

NX, NZ, NC = 4, 8, 2
NF = NX * NZ * NC
WIDTH = 5120
HEADS = 8
HEAD = 128
ROWS = 128
SHARD = WIDTH // NF
BLOCK = 8
HALO = 4
BLOCKS = ROWS // BLOCK
KTOK = NF * (BLOCK + HALO)
QTOK = NX * BLOCK
PAD = NX * HALO
X_ORDER = (0, -1, 1, 2)
Z_ORDER = (0, -1, 1, -2, 2, -3, 3, 4)
NEAR = 5

eps = 1e-06
rope_base = 1000000.0
BF = jnp.bfloat16
F32 = jnp.float32


def shift(value, axis, size, by):
    return lax.ppermute(value, axis, [(i, (i + by) % size) for i in range(size)])


def rollout_starts(lengths, owner, tokens):
    index = jnp.arange(lengths.shape[0], dtype=jnp.int32)
    earlier = (owner[None, :] < owner[:, None]) | (owner[None, :] == owner[:, None]) & (
        index[None, :] < index[:, None]
    )
    offset = jnp.sum(jnp.where(earlier, lengths[None, :], 0), axis=1)
    return jnp.max(jnp.where(offset[None, :] <= tokens[:, None], offset[None, :], 0), axis=1)


def rope_tables(positions):
    half = HEAD // 2
    steps = jnp.arange(half, dtype=F32) * (2.0 / HEAD)
    inverse = jnp.power(F32(rope_base), -steps)
    angles = positions.astype(F32)[:, None] * inverse[None, :]
    cosine = jnp.cos(angles)
    sine = jnp.sin(angles)
    return (
        jnp.concatenate([cosine, cosine], axis=1),
        jnp.concatenate([-sine, sine], axis=1),
    )


def normed_rope(value, gain, cosine, sine):
    mean_square = jnp.mean(value * value, axis=-1, keepdims=True)
    value = value * lax.rsqrt(mean_square + eps) * gain
    return value * cosine + pltpu.roll(value, HEAD // 2, 1) * sine


def pack_kernel(place, key, value, *out):
    for k, by in enumerate(X_ORDER):
        head = lax.rem(place[0] - by + NX, NX)
        lanes = pl.ds(pl.multiple_of(head * HEAD, HEAD), HEAD)
        out[k][:, :HEAD] = key[:, lanes]
        out[k][:, HEAD:] = value[:, lanes]


def stack_kernel(place, *refs):
    for k, by in enumerate(X_ORDER):
        refs[-1][lax.rem(place[0] + by + NX, NX)] = refs[k][...]


def norm_kernel(hidden, gain, out):
    block = 16

    def body(i, carry):
        rows = pl.ds(pl.multiple_of(i * block, block), block)
        value = hidden[rows, :].astype(F32)
        mean_square = jnp.mean(value * value, axis=-1, keepdims=True)
        value = value * lax.rsqrt(mean_square + eps) * gain[...]
        out[rows, :] = value.astype(BF)
        return carry

    lax.fori_loop(0, ROWS // block, body, 0)


def project(x, w, gain, cosine, sine):
    raw = jnp.dot(x, w, preferred_element_type=F32)
    return normed_rope(raw[:, :HEAD], gain, cosine, sine), raw[:, HEAD:]


def first_kernel(
    place,
    own,
    left,
    right,
    mine,
    mine2,
    other,
    other2,
    gain,
    cosine,
    sine,
    out,
    weight,
    tokens,
    sem,
    token_sem,
):
    z, c = place[1], place[2]
    copies = []
    for k, by in enumerate(Z_ORDER):
        at = lax.rem(z + by + NZ, NZ)
        near = k < NEAR
        for which, core in (((mine, mine2)[k >= NEAR], c), ((other, other2)[k >= NEAR], 1 - c)):
            copies.append(
                pltpu.make_async_copy(
                    which.at[k if near else k - NEAR], weight.at[:, at, core], sem.at[len(copies)]
                )
            )
    loads = []
    for k, chunk in enumerate((own, left, right)):
        loads.append(pltpu.make_async_copy(chunk, tokens.at[k], token_sem.at[k]))
    for copy in copies + loads:
        copy.start()
    for copy in copies:
        copy.wait()
    w = weight[...].reshape(WIDTH, 2 * HEAD)
    for load in loads:
        load.wait()

    def body(k, carry):
        rows = pl.ds(pl.multiple_of(k * ROWS, ROWS), ROWS)
        key, value = project(tokens[k], w, gain[...], cosine[rows, :], sine[rows, :])
        out[k, 0] = key
        out[k, 1] = value
        return carry

    lax.fori_loop(0, NX - 1, body, 0)


def second_kernel(far_a, far_b, weight, made, gain, cosine, sine, out, keep_k, keep_v):
    w = weight[...].reshape(WIDTH, 2 * HEAD)
    x = jnp.concatenate([far_a[...], far_b[...]], axis=0)
    rows = pl.ds((NX - 1) * ROWS, ROWS)
    far = project(x, w, gain[...], cosine[rows, :], sine[rows, :])
    for side, keep in enumerate((keep_k, keep_v)):
        for k in range(NX - 1):
            keep[pl.ds(k, ROWS, stride=NX), :] = made[k, side]
        keep[pl.ds(NX - 1, ROWS, stride=NX), :] = far[side]
        out[:, pl.ds(side * HEAD, HEAD)] = keep[...].astype(BF)


def split_kernel(place, q, *out):
    width = HEADS * HEAD
    for k, by in enumerate(X_ORDER):
        x = lax.rem(place[0] - by + NX, NX)
        out[k][...] = q[:, pl.ds(pl.multiple_of(x * width, width), width)]


def join_kernel(place, *refs):
    out = refs[-1]
    width = HEADS * HEAD
    for k, by in enumerate(X_ORDER):
        x = lax.rem(place[0] - by + NX, NX)
        out[:, pl.ds(pl.multiple_of(x * width, width), width)] = refs[k][...]


def prepare_kernel(q0, q1, q2, q3, gain, cosine, sine, out):
    def body(h, carry):
        lanes = pl.ds(pl.multiple_of(h * HEAD, HEAD), HEAD)
        done = []
        for k, q in enumerate((q0, q1, q2, q3)):
            rows = pl.ds(k * ROWS, ROWS)
            value = q[:, lanes].astype(F32)
            done.append(normed_rope(value, gain[...], cosine[rows, :], sine[rows, :]))
        for b in range(BLOCKS):
            rows = slice(b * BLOCK, (b + 1) * BLOCK)
            block = jnp.concatenate([value[rows] for value in done], axis=0)
            at = pl.ds(pl.multiple_of(h * QTOK, QTOK), QTOK)
            out[b, at, :] = block.astype(BF)
        return carry

    lax.fori_loop(0, HEADS, body, 0)


def attend_kernel(
    place,
    q_in,
    mine,
    mine2,
    mine3,
    other,
    other2,
    other3,
    token_in,
    start_in,
    key_token,
    o0,
    o1,
    o2,
    o3,
    kv,
    q,
    token,
    start,
    probs,
    scores,
    mixed,
    sem,
):
    copies = [
        pltpu.make_async_copy(q_in, q, sem.at[0]),
        pltpu.make_async_copy(token_in, token, sem.at[1]),
        pltpu.make_async_copy(start_in, start, sem.at[2]),
    ]
    for side, group in enumerate(((mine, mine2, mine3), (other, other2, other3))):
        at = 0
        for part in group:
            count = part.shape[0]
            copies.append(
                pltpu.make_async_copy(
                    part,
                    kv.at[side, pl.ds(at, count), pl.ds(PAD, NX * ROWS), :],
                    sem.at[len(copies)],
                )
            )
            at += count
    for copy in copies:
        copy.start()
    kv[:, :, :PAD, :] = jnp.zeros((NC, NZ, PAD, 2 * HEAD), BF)
    for copy in copies:
        copy.wait()
    scale = np.float32(1.0 / np.sqrt(HEAD))

    def window(b, side):
        rows = pl.ds(pl.multiple_of(b * QTOK, QTOK), PAD + QTOK)
        return kv[:, :, rows, pl.ds(side * HEAD, HEAD)].reshape(KTOK, HEAD)

    def score(b, slot):
        scores[slot] = lax.dot_general(
            q[b], window(b, 0), (((1,), (1,)), ((), ())), preferred_element_type=F32
        )

    score(0, 0)

    def body(i, carry):
        for j in range(4):
            b, slot = 4 * i + j, j % 2
            score(jnp.minimum(b + 1, BLOCKS - 1), 1 - slot)
            key = key_token[...] + b * BLOCK * NF
            seen = (key >= start[b, :, :1]) & (key <= token[b, :, :1])
            bias = jnp.where(seen, 0.0, -jnp.inf)
            for h in range(HEADS):
                head = pl.ds(h * QTOK, QTOK)
                s = scores[slot, head, :] * scale + bias
                weights = jnp.exp(s - jnp.max(s, axis=1, keepdims=True))
                total = jnp.sum(weights, axis=1, keepdims=True)
                probs[slot, head, :] = (weights * (1.0 / total)).astype(BF)
            m = jnp.dot(probs[slot], window(b, 1), preferred_element_type=F32)
            rows = pl.ds(pl.multiple_of(b * BLOCK, BLOCK), BLOCK)
            for h in range(HEADS):
                for k in range(NX):
                    at = h * QTOK + k * BLOCK
                    mixed[k, rows, pl.ds(h * HEAD, HEAD)] = m[at : at + BLOCK]
        return carry

    lax.fori_loop(0, BLOCKS // 4, body, 0)
    for k, out in enumerate((o0, o1, o2, o3)):
        out[...] = mixed[k].astype(BF)


def per_device(
    hidden_rows,
    queries,
    norm_gain,
    query_gain,
    key_norm_gain,
    key_matrix,
    value_matrix,
    lengths,
    owner,
):
    x, z, c = (lax.axis_index(a).astype(jnp.int32) for a in ("x", "z", "core"))
    zc = z * NC + c
    place = jnp.stack([x, z, c])
    vmem = pl.BlockSpec(memory_space=pltpu.VMEM)
    anywhere = pl.BlockSpec(memory_space=pl.ANY)
    smem = pl.BlockSpec(memory_space=pltpu.SMEM)
    rows = jnp.arange(ROWS, dtype=jnp.int32)
    chunk_x = jnp.stack([(x + by + NX) % NX for by in X_ORDER])
    token = rows[None, :] * NF + chunk_x[:, None] * (NZ * NC) + zc
    start = rollout_starts(lengths, owner, token.reshape(-1))
    key_cos, key_sin = rope_tables(token.reshape(-1) - start)

    def blocked(value):
        value = value.reshape(NX, BLOCKS, BLOCK).transpose(1, 0, 2)
        return jnp.broadcast_to(value.reshape(BLOCKS, QTOK, 1), (BLOCKS, QTOK, HEAD))

    core = jnp.stack([c, 1 - c])
    around = jnp.stack([(z + by + NZ) % NZ for by in Z_ORDER])
    key_rows = jnp.arange(-HALO, BLOCK, dtype=jnp.int32)
    key_token = (
        key_rows[None, None, :, None] * NF
        + chunk_x[None, None, None, :] * (NZ * NC)
        + around[None, :, None, None] * NC
        + core[:, None, None, None]
    ).reshape(1, KTOK)

    seen_by = (blocked(token), blocked(start), key_token)

    bar = lax.optimization_barrier
    packed = pl.pallas_call(
        pack_kernel,
        in_specs=[smem, vmem, vmem],
        out_specs=[vmem] * NX,
        out_shape=[jax.ShapeDtypeStruct((SHARD, 2 * HEAD), BF)] * NX,
        name="pack_weights",
    )(place, key_matrix, value_matrix)
    hidden_rows, packed = bar((hidden_rows, packed))
    own = pl.pallas_call(
        norm_kernel,
        in_specs=[vmem, vmem],
        out_specs=vmem,
        out_shape=jax.ShapeDtypeStruct((ROWS, WIDTH), BF),
        name="norm_hidden",
    )(hidden_rows, norm_gain.reshape(1, WIDTH))
    piece = pl.pallas_call(
        stack_kernel,
        in_specs=[smem] + [vmem] * NX,
        out_specs=vmem,
        out_shape=jax.ShapeDtypeStruct((NX, SHARD, 2 * HEAD), BF),
        name="stack_weights",
    )(place, packed[0], *[shift(packed[k], "x", NX, -X_ORDER[k]) for k in range(1, NX)])

    parts = pl.pallas_call(
        split_kernel,
        in_specs=[smem, vmem],
        out_specs=[vmem] * NX,
        out_shape=[jax.ShapeDtypeStruct((ROWS, HEADS * HEAD), BF)] * NX,
        name="split_queries",
    )(place, queries)
    piece, own = bar((piece, own))
    left = shift(own, "x", NX, 1)
    right = shift(own, "x", NX, -1)

    cut = ROWS // 2
    pieces = [piece]
    up = down = piece
    for step in range(NZ // 2 - 1):
        up = shift(up, "z", NZ, 1)
        down = shift(down, "z", NZ, -1)
        if step == 0:
            up, down, seen_by, key_cos, key_sin, parts = bar(
                (up, down, seen_by, key_cos, key_sin, parts)
            )
        if step == 2:
            up, down, left, right = bar((up, down, left, right))
            far_a = shift(left[:cut], "x", NX, 1)
            far_b = shift(right[cut:], "x", NX, -1)
        pieces += [up, down]
    half = NX // 2
    last_a = shift(up[:half], "z", NZ, 1)
    last_b = shift(down[half:], "z", NZ, -1)
    pieces.append(jnp.concatenate([last_a, last_b], axis=0))
    mine, mine2 = jnp.stack(pieces[:NEAR]), jnp.stack(pieces[NEAR:])
    mine2, far_a, far_b = bar((mine2, far_a, far_b))
    other, other2 = shift(mine, "core", NC, 1), shift(mine2, "core", NC, 1)

    parts, far_a, far_b = bar((parts, far_a, far_b))
    got = [parts[0]] + [shift(parts[k], "x", NX, -X_ORDER[k]) for k in range(1, NX)]

    key_gain = key_norm_gain.reshape(1, HEAD)
    made_first, weight = pl.pallas_call(
        first_kernel,
        in_specs=[smem] + [anywhere] * 7 + [vmem] * 3,
        out_specs=[vmem] * 2,
        out_shape=[
            jax.ShapeDtypeStruct((NX - 1, 2, ROWS, HEAD), F32),
            jax.ShapeDtypeStruct((NX, NZ, NC, SHARD, 2 * HEAD), BF),
        ],
        scratch_shapes=[
            pltpu.VMEM((NX - 1, ROWS, WIDTH), BF),
            pltpu.SemaphoreType.DMA((2 * NZ,)),
            pltpu.SemaphoreType.DMA((NX - 1,)),
        ],
        compiler_params=pltpu.CompilerParams(vmem_limit_bytes=32 * 2**20),
        name="project_first",
    )(place, own, left, right, mine, mine2, other, other2, key_gain, key_cos, key_sin)
    made_kv = pl.pallas_call(
        second_kernel,
        in_specs=[vmem] * 7,
        out_specs=vmem,
        out_shape=jax.ShapeDtypeStruct((NX * ROWS, 2 * HEAD), BF),
        scratch_shapes=[pltpu.VMEM((NX * ROWS, HEAD), F32)] * 2,
        compiler_params=pltpu.CompilerParams(vmem_limit_bytes=32 * 2**20),
        name="project_last",
    )(far_a, far_b, weight, made_first, key_gain, key_cos, key_sin)
    def prepare(got):
        return pl.pallas_call(
            prepare_kernel,
            in_specs=[vmem] * 7,
            out_specs=vmem,
            out_shape=jax.ShapeDtypeStruct((BLOCKS, HEADS * QTOK, HEAD), BF),
            compiler_params=pltpu.CompilerParams(vmem_limit_bytes=32 * 2**20),
            name="prepare_queries",
        )(*got, query_gain.reshape(1, HEAD), key_cos, key_sin)

    up = down = made_kv
    first, second = [made_kv], []
    for step in range(NZ // 2 - 1):
        up = shift(up, "z", NZ, 1)
        down = shift(down, "z", NZ, -1)
        if step == 0:
            up, down, got = bar((up, down, got))
            ready = prepare(got)
        (first if step < 2 else second).extend([up, down])
    half = NX * ROWS // 2
    third = jnp.concatenate(
        [shift(up[:half], "z", NZ, 1), shift(down[half:], "z", NZ, -1)], axis=0
    )
    groups = [jnp.stack(first), jnp.stack(second), third[None]]
    crossed = [shift(group, "core", NC, 1) for group in groups]

    mixed = pl.pallas_call(
        attend_kernel,
        in_specs=[smem] + [anywhere] * 9 + [vmem],
        out_specs=[vmem] * NX,
        out_shape=[jax.ShapeDtypeStruct((ROWS, HEADS * HEAD), BF)] * NX,
        scratch_shapes=[
            pltpu.VMEM((NC, NZ, PAD + NX * ROWS, 2 * HEAD), BF),
            pltpu.VMEM((BLOCKS, HEADS * QTOK, HEAD), BF),
            pltpu.VMEM((BLOCKS, QTOK, HEAD), jnp.int32),
            pltpu.VMEM((BLOCKS, QTOK, HEAD), jnp.int32),
            pltpu.VMEM((2, HEADS * QTOK, KTOK), BF),
            pltpu.VMEM((2, HEADS * QTOK, KTOK), F32),
            pltpu.VMEM((NX, ROWS, HEADS * HEAD), F32),
            pltpu.SemaphoreType.DMA((9,)),
        ],
        compiler_params=pltpu.CompilerParams(vmem_limit_bytes=40 * 2**20),
        name="attend",
    )(place, ready, *groups, *crossed, *seen_by)
    back = [mixed[0]] + [shift(mixed[k], "x", NX, X_ORDER[k]) for k in range(1, NX)]
    return pl.pallas_call(
        join_kernel,
        in_specs=[smem] + [vmem] * NX,
        out_specs=vmem,
        out_shape=jax.ShapeDtypeStruct((ROWS, NX * HEADS * HEAD), BF),
        name="join_heads",
    )(place, *back)


def solution(mesh):
    grid = Mesh(mesh.devices.reshape(NX, NZ, NC, mesh.devices.shape[1]), ("x", "z", "core", "rep"))
    fsdp = ("x", "z", "core")
    whole = P(("rep",) + fsdp, None)
    placed = (whole, whole, P(), P(), P(), P(fsdp, None), P(fsdp, None), P("rep"), P("rep"))
    return jax.shard_map(
        per_device, mesh=grid, in_specs=placed, out_specs=whole, check_vma=False
    )
```
